256 devices in a mesh: col: 16 (over x, y_lo, core), rep: 16 (over y_hi, z).
Axes of the slice: x: 4, y: 4 (y_hi: 2, y_lo: 2; y = y_hi * 2 + y_lo), z: 8, core: 2. Of those that a mesh axis runs over, the one named last changes fastest.
Arguments:
- features: bfloat16 [32768, 512], P(('col', 'rep')), may hold values from -24 to 24
- reorder: int32 [256, 128], P(('col', 'rep')), may hold values from 0 to 127, each once within a row
- weight: bfloat16 [512, 512], replicated, may hold values from -0.25 to 0.25
- adjacency: bfloat16 [16, 16, 16, 16, 128, 128], P('col', 'rep'), may hold values from 0 to 10, as said below
- tile_block: int32 [16, 16, 16, 16], P('col', 'rep'), may hold values from 0 to 15
- live_counts: int32 [16, 16, 16], P('col', 'rep'), may hold values from 8 to 16, as said below
- grad_out: bfloat16 [32768, 512], P(('col', 'rep')), may hold values from -6 to 6
Outputs:
- activated: bfloat16 [32768, 512], P(('col', 'rep'))
- weight_grad: float32 [512, 512], P(('col', 'rep'))
- feature_grad: bfloat16 [32768, 512], P(('col', 'rep'))
The draws below stay inside these ranges and needn't reach their ends.
Inputs may be any that keep to these rules, and one draw needn't show every extreme that they name: `adjacency`: edge weights are nonnegative. `live_counts`: some triple has all 16 slots live in every draw.
All inputs are finite; a program needn't handle non-finite values.
Results may differ from the reference program's by a relative error of at most 0.006.
Values may be sent and summed in bfloat16 or wider, within the bound.
A program may use at most 64 MiB of HBM per device.

```python
import math
import jax
import jax.numpy as jnp
from jax import lax

F = 512
TILE = 128
TPK = 16
GROUPS = 16
REPS = 16
SHARDS = 256
NODES = 32768


def draw_adjacency(key, part):
    full_shape = (GROUPS, REPS, GROUPS, TPK, TILE, TILE)
    key_base, key_rows, key_cols = jax.random.split(key, 3)
    base_value = jax.random.uniform(key_base, full_shape, jnp.float32)
    row_scale = jnp.exp(jax.random.uniform(key_rows, full_shape[:-1] + (1,), jnp.float32) * math.log(10.0))
    col_scale = jnp.exp(jax.random.uniform(key_cols, full_shape[:-2] + (1, TILE), jnp.float32) * math.log(10.0))
    return (0.1 * base_value * row_scale * col_scale).astype(jnp.bfloat16)


def draw_live_counts(key, part):
    full_shape = (GROUPS, REPS, GROUPS)
    key_limit, key_value, key_place = jax.random.split(key, 3)
    lowest = max(TPK // 2, 1)
    limits = jax.random.randint(key_limit, (GROUPS, 1, 1), lowest + 1, TPK + 1)
    raw_bits = jax.random.randint(key_value, full_shape, 0, 65536)
    counts_drawn = lowest + raw_bits % (limits - lowest + 1)
    chosen = jax.random.randint(key_place, (), 0, GROUPS * REPS * GROUPS)
    flat_index = jnp.arange(GROUPS * REPS * GROUPS, dtype=jnp.int32).reshape(full_shape)
    return jnp.where(flat_index == chosen, TPK, counts_drawn).astype(jnp.int32)


def with_ends(entries, own_key, low, largest):
    spot = [jax.random.randint(jax.random.fold_in(own_key, axis), (), 0, length) for axis, length in enumerate(entries.shape)]
    main_axis = entries.shape.index(max(entries.shape))
    next_to = spot[:main_axis] + [(spot[main_axis] + 1) % entries.shape[main_axis]] + spot[main_axis + 1:]
    return entries.at[tuple(spot)].set(low).at[tuple(next_to)].set(largest)


def spiked(array, stream_key, source, target, blocks, factor):
    def block_of(axis_at):
        return (jnp.arange(array.shape[axis_at]) // (array.shape[axis_at] // blocks)).reshape((-1,) + (1,) * (array.ndim - 1 - axis_at))

    one_side = jax.random.permutation(stream_key, blocks)[block_of(target)]
    far = (block_of(target) + blocks // 2) % blocks
    return jnp.where((block_of(source) == one_side) | (block_of(source) == far), factor * array, array)


def block_levels(own_key, shape, shards, smallest, high):
    factor_of = 1.0
    for position, blocks in shards:
        heights = jax.random.uniform(jax.random.fold_in(jax.random.fold_in(own_key, 6), position), (blocks,), jnp.float32, smallest / len(shards), high / len(shards))
        factor_of = factor_of * jnp.repeat(jnp.exp(heights), shape[position] // blocks).reshape((-1,) + (1,) * (len(shape) - 1 - position))
    return factor_of


def centred(stream_key, dims, width, most, cuts=(), kind=jnp.bfloat16):
    factor_of = block_levels(stream_key, dims, cuts, -0.22, 0.18) if cuts else 1.0
    values = jax.random.normal(stream_key, dims, jnp.float32) * width * factor_of
    return jnp.minimum(jnp.maximum(values, -most), most).astype(kind)


def gaussian_with(own_key, extent, scale, bound, cuts, heavy, held_as=jnp.bfloat16):
    result = scale * jax.random.normal(own_key, extent, jnp.float32)
    if cuts:
        result = result * block_levels(own_key, extent, cuts, -0.22, 0.18)
    return jnp.clip(spiked(result, jax.random.fold_in(own_key, 3), *heavy), -bound, bound).astype(held_as)


def setup_inputs(seed: int = 0) -> dict:
    seeds = jax.random.split(jax.random.key(seed), 8)
    return {
        "features": gaussian_with(seeds[0], (NODES, F), 1.0, 24.0, ((0, 256),), (0, 1, 256, 6.0)),
        "reorder": jax.vmap(lambda own: jax.random.permutation(own, TILE))(jax.random.split(seeds[1], SHARDS)).reshape((SHARDS, TILE)).astype(jnp.int32),
        "weight": centred(seeds[2], (F, F), F ** -0.5, 0.25),
        "adjacency": draw_adjacency(jax.random.fold_in(seeds[7], 71), 0),
        "tile_block": with_ends(jax.random.randint(seeds[4], (GROUPS, REPS, GROUPS, TPK), 0, REPS), jax.random.fold_in(seeds[4], 1), 0, REPS - 1).astype(jnp.int32),
        "live_counts": draw_live_counts(jax.random.fold_in(seeds[7], 71), 0),
        "grad_out": centred(seeds[6], (NODES, F), 1.0, 6.0, ((0, 256),)),
    }


def reference(features, reorder, weight, adjacency, tile_block, live_counts, grad_out):
    node_index = (jnp.arange(SHARDS, dtype=jnp.int32)[:, None] * TILE + reorder).reshape(-1).astype(jnp.int32)
    reordered = features[node_index]
    projected = jnp.dot(reordered, weight, preferred_element_type=jnp.float32).astype(jnp.bfloat16)
    blocks_all = projected.reshape(GROUPS, REPS, TILE, F)
    live_mask = jnp.arange(TPK, dtype=jnp.int32) < live_counts[..., None]

    def forward_group(carried, group_id):
        sums_acc, degree_acc = carried
        tiles_g = adjacency[group_id]
        ids_g = tile_block[group_id]
        live_g = live_mask[group_id]
        panel_rows = blocks_all[group_id]

        def per_copy(copy_id):
            tile_set = tiles_g[copy_id].astype(jnp.float32)
            gathered = jnp.where(live_g[copy_id][..., None, None], panel_rows[ids_g[copy_id]].astype(jnp.float32), 0.0)
            contrib = jnp.einsum('ktij,ktjf->kif', tile_set, gathered)
            row_part = lax.optimization_barrier(jnp.sum(jnp.where(live_g[copy_id][..., None], lax.optimization_barrier(jnp.sum(tile_set, axis=3)), 0.0), axis=1))
            return (contrib, row_part)
        contribs, row_parts = lax.map(per_copy, jnp.arange(REPS, dtype=jnp.int32))
        return ((sums_acc + jnp.swapaxes(contribs, 0, 1), degree_acc + jnp.swapaxes(row_parts, 0, 1)), None)
    start_sums = jnp.zeros((GROUPS, REPS, TILE, F), jnp.float32)
    start_degree = jnp.zeros((GROUPS, REPS, TILE), jnp.float32)
    (sums_acc, degree_acc), _ = lax.scan(forward_group, (start_sums, start_degree), jnp.arange(GROUPS, dtype=jnp.int32))
    scale = lax.rsqrt(1.0 + degree_acc.reshape(NODES))[:, None]
    pre_act = sums_acc.reshape(NODES, F) * scale + projected.astype(jnp.float32)
    activated = jax.nn.silu(pre_act).astype(jnp.bfloat16)
    sigmoid_val = jax.nn.sigmoid(pre_act)
    pre_grad = grad_out.astype(jnp.float32) * sigmoid_val * (1.0 + pre_act * (1.0 - sigmoid_val))
    scaled_rows = (pre_grad * scale).astype(jnp.bfloat16).reshape(GROUPS, REPS, TILE, F)

    def backward_group(group_id):
        tiles_g = adjacency[group_id]
        ids_g = tile_block[group_id]
        live_g = live_mask[group_id]

        def per_copy(copy_id):
            tile_set = tiles_g[copy_id].astype(jnp.float32)
            src_rows = jnp.take(scaled_rows, copy_id, axis=1).astype(jnp.float32)
            contrib = jnp.einsum('ktij,kif->ktjf', tile_set, src_rows)
            onehot = ((ids_g[copy_id][..., None] == jnp.arange(REPS, dtype=jnp.int32)) & live_g[copy_id][..., None]).astype(jnp.float32)
            return jnp.einsum('ktb,ktjf->bjf', onehot, contrib)
        return lax.optimization_barrier(jnp.sum(lax.map(per_copy, jnp.arange(REPS, dtype=jnp.int32)), axis=0))
    column_part = lax.map(backward_group, jnp.arange(GROUPS, dtype=jnp.int32)).reshape(NODES, F)
    back_rows = (column_part + pre_grad).astype(jnp.bfloat16)
    weight_grad = jnp.dot(reordered.T, back_rows, preferred_element_type=jnp.float32) * (1.0 / math.sqrt(NODES))
    input_rows = jnp.dot(back_rows, weight.T, preferred_element_type=jnp.float32).astype(jnp.bfloat16)
    feature_grad = jnp.zeros((NODES, F), jnp.bfloat16).at[node_index].set(input_rows)
    return (activated, weight_grad, feature_grad)
```

```python
import functools
import math

import jax
import jax.numpy as jnp
from jax import lax
from jax.experimental import pallas as pl
from jax.experimental.pallas import tpu as pltpu
from jax.sharding import PartitionSpec as P

F32, BF16 = jnp.float32, jnp.bfloat16


def dot(a, b):
    return jnp.dot(a, b, preferred_element_type=F32)


def slab_kernel(block_ref, count_ref, tiles_ref, slab_ref, degree_ref, acc):
    k = pl.program_id(0)
    acc[...] = jnp.zeros_like(acc)

    def add(t, sums):
        b = block_ref[k, t]
        tile = tiles_ref[t].astype(F32)
        acc[b] = acc[b] + tile
        return sums + tile

    sums = lax.fori_loop(0, count_ref[k], add, jnp.zeros(acc.shape[1:], F32))
    slab_ref[...] = acc[...].astype(BF16)
    degree_ref[...] = jnp.broadcast_to(
        jnp.sum(sums.T, axis=0, keepdims=True), degree_ref.shape
    )


def dense_slab(tile_block, live_counts, adjacency):
    _, _, rows, slots, tile, _ = adjacency.shape
    blocks = 16
    return pl.pallas_call(
        slab_kernel,
        grid_spec=pltpu.PrefetchScalarGridSpec(
            num_scalar_prefetch=2,
            grid=(rows,),
            in_specs=[
                pl.BlockSpec(
                    (None, None, None, slots, tile, tile),
                    lambda k, *_: (0, 0, k, 0, 0, 0),
                )
            ],
            out_specs=[
                pl.BlockSpec((blocks, tile, tile), lambda k, *_: (0, k, 0)),
                pl.BlockSpec((None, 8, tile), lambda k, *_: (k, 0, 0)),
            ],
            scratch_shapes=[pltpu.VMEM((blocks, tile, tile), F32)],
        ),
        out_shape=[
            jax.ShapeDtypeStruct((blocks, rows * tile, tile), BF16),
            jax.ShapeDtypeStruct((rows, 8, tile), F32),
        ],
    )(tile_block, live_counts, adjacency)


GATHER = ["y0"] + [
    d + n for d in "pm" for n in ("w1", "w2", "w3", "w4", "o3", "o4", "y1", "y2")
]
FORWARD = [f"c{j}" for j in range(8)] + ["a", "b+", "b-", "c+", "c-", "d", "e+", "e-"]
BACK = [f"c{j}" for j in range(8)] + ["x+", "x-", "y", "h+", "h-", "y2", "n+", "n-"]
REDUCE = GATHER
SETS = [("g", GATHER), ("f", FORWARD), ("b", BACK), ("r", REDUCE)]
INDEX = {s + n: i for i, (s, n) in enumerate((s, n) for s, names in SETS for n in names)}
N_SEMS = len(INDEX)
PLACES = [(2, 1), (1, 1), (3, 1), (2, 0), (1, 0), (3, 0), (0, 1), (0, 0)]


def layer_kernel(
    feat_ref, order_ref, w_ref, slab_hbm, degree_ref, grad_ref,
    act_ref, wgrad_ref, fgrad_ref,
    slab, panel, projected, acc, stage_f, land_f, rows_t, totals, totals_low,
    stage_r, land_r, half_r, wsend, wland, wown, wsend2, wland2,
    slab_sem, send_sem, recv_sem, wsend_sem, wrecv_sem,
):
    tile, width = feat_ref.shape
    c, r = lax.axis_index("col"), lax.axis_index("rep")
    x, yl, core = c // 4, (c // 2) % 2, c % 2
    yh, z = r // 8, r % 8

    def group(dx, dy, dc):
        return ((x + dx) % 4) * 4 + ((yl + dy) % 2) * 2 + (core + dc) % 2

    def block(p, d):
        return ((yh + p) % 2) * 8 + (z + d + 8) % 8

    up, down, over = (c, block(0, 1)), (c, block(0, -1)), (c, block(1, 0))
    right, left, beside = (group(1, 0, 0), r), (group(3, 0, 0), r), (group(0, 1, 0), r)
    partner = (group(0, 0, 1), r)

    slab_copy = pltpu.make_async_copy(slab_hbm, slab, slab_sem)
    slab_copy.start()

    barrier = pltpu.get_barrier_semaphore()
    for device in (up, down, over, right, left, beside, partner):
        pl.semaphore_signal(barrier, 1, device_id=device)

    place = (
        lax.broadcasted_iota(jnp.int32, (tile, tile), 0) == order_ref[...]
    ).astype(F32)
    own = block(0, 0)
    panel[own] = dot(place.T.astype(BF16), feat_ref[...]).astype(BF16)

    pl.semaphore_wait(barrier, 7)
    copies = {}

    def send(name, src, dst, device):
        i = INDEX[name]
        copy = pltpu.make_async_remote_copy(
            src, dst, send_sem.at[i], recv_sem.at[i], device_id=device
        )
        copy.start()
        copies[name] = copy

    def arrived(name):
        copies[name].wait_recv()

    def pass_on(name, p, d, device, half=None):
        ref = panel.at[block(p, d)]
        if half is not None:
            ref = ref.at[pl.ds(half * tile // 2, tile // 2)]
        send("g" + name, ref, ref, device)

    def consume(b1, b2, first=False):
        for b in (b1, b2):
            projected[b] = dot(panel[b], w_ref[...]).astype(BF16)
        pair = jnp.concatenate([projected[b1], projected[b2]], axis=0)

        @pl.loop(0, slab.shape[1] // 512)
        def _(i):
            rows = pl.ds(pl.multiple_of(i * 512, 512), 512)
            part = dot(jnp.concatenate([slab[b1, rows], slab[b2, rows]], axis=1), pair)
            acc[rows] = part if first else acc[rows] + part

    ways = (("p", -1, up, 0), ("m", 1, down, 1))
    for way, s, device, h in ways:
        pass_on(way + "w1", 0, 0, device)
    pass_on("y0", 0, 0, over)
    for way, s, device, h in ways:
        arrived("g" + way + "w1")
        pass_on(way + "w2", 0, s, device)
        pass_on(way + "y1", 0, s, over)
    arrived("gy0")
    slab_copy.wait()
    consume(own, block(1, 0), first=True)
    for way, s, device, h in ways:
        arrived("g" + way + "w2")
        pass_on(way + "w3", 0, 2 * s, device)
        pass_on(way + "y2", 0, 2 * s, over)
    consume(block(0, 1), block(0, -1))
    for way, s, device, h in ways:
        arrived("g" + way + "w3")
        pass_on(way + "w4", 0, 3 * s, device, h)
        arrived("g" + way + "y1")
    consume(block(0, 2), block(0, -2))
    consume(block(1, 1), block(1, -1))
    for way, s, device, h in ways:
        arrived("g" + way + "y2")
        pass_on(way + "o3", 1, 2 * s, device)
    consume(block(0, 3), block(0, -3))
    for way, s, device, h in ways:
        arrived("g" + way + "w4")
        arrived("g" + way + "o3")
        pass_on(way + "o4", 1, 3 * s, device, h)
    consume(block(1, 2), block(1, -2))
    consume(block(1, 3), block(1, -3))
    for way, s, device, h in ways:
        arrived("g" + way + "o4")
    consume(block(0, 4), block(1, 4))

    def mine(dx, dy, dc=0):
        k = group(dx, dy, dc)
        rows = acc[pl.ds(pl.multiple_of(k * tile, tile), tile)]
        return rows, degree_ref[k][0:1]

    def pack(slot, value):
        rows, degree = value
        high = degree.astype(BF16)
        low = (degree - high.astype(F32)).astype(BF16)
        stage_f[slot, 0:tile] = rows.astype(BF16)
        stage_f[slot, tile : tile + 16] = jnp.concatenate(
            [
                jnp.broadcast_to(part, (16, tile))
                for part in (high, low, jnp.zeros_like(high), jnp.zeros_like(high))
            ],
            axis=1,
        )

    def degree_in(slot):
        tail = land_f[slot, tile : tile + 16].astype(F32)
        return tail[0:1, 0:tile] + tail[0:1, tile : 2 * tile]

    def plus(value, slot):
        rows, degree = value
        return rows + land_f[slot, 0:tile].astype(F32), degree + degree_in(slot)

    def ship(name, slot, device, lo=0, hi=tile + 16):
        span = pl.ds(lo, hi - lo)
        i = FORWARD.index(name)
        send("f" + name, stage_f.at[slot, span], land_f.at[i, span], device)

    at = {name: i for i, name in enumerate(FORWARD)}
    for j, (dx, dy) in enumerate(PLACES):
        pack(j, mine(dx, dy, 1))
        ship(f"c{j}", j, partner)

    def both(dx, dy):
        j = PLACES.index((dx, dy))
        arrived(f"fc{j}")
        return plus(mine(dx, dy), j)

    half = tile // 2
    pack(at["a"], both(2, 1))
    ship("a", at["a"], beside)
    for s, dx, device in (("+", 1, right), ("-", 3, left)):
        pack(at["b" + s], both(dx, 1))
        ship("b" + s, at["b" + s], device)
    far = both(2, 0)
    arrived("fa")
    pack(at["c+"], plus(far, at["a"]))
    ship("c+", at["c+"], right, 0, half)
    ship("c-", at["c+"], left, half, tile + 16)
    near = both(0, 1)
    for s in "+-":
        arrived("fb" + s)
        near = plus(near, at["b" + s])
    pack(at["d"], near)
    ship("d", at["d"], beside)
    rows, degree = both(1, 0)
    arrived("fc+")
    top = rows[:half] + land_f[at["c+"], 0:half].astype(F32)
    pack(at["e+"], (jnp.concatenate([top, rows[half:]], axis=0), degree))
    ship("e+", at["e+"], right)
    rows, degree = both(3, 0)
    arrived("fc-")
    bottom = rows[half:] + land_f[at["c-"], half:tile].astype(F32)
    pack(
        at["e-"],
        (jnp.concatenate([rows[:half], bottom], axis=0), degree + degree_in(at["c-"])),
    )
    ship("e-", at["e-"], left)
    whole = both(0, 0)
    for name in ("d", "e+", "e-"):
        arrived("f" + name)
        whole = plus(whole, at[name])

    summed, degree = whole
    scale = lax.rsqrt(1.0 + jnp.broadcast_to(degree, (tile, tile)).T)
    scale = jnp.concatenate([scale] * (width // tile), axis=1)
    pre_act = summed * scale + projected[own].astype(F32)
    sigmoid = 1.0 / (1.0 + jnp.exp(-pre_act))
    pre_grad = grad_ref[...].astype(F32) * sigmoid * (1.0 + pre_act * (1.0 - sigmoid))
    pre_grad_t = pre_grad.T
    rows_t[c] = (pre_grad * scale).T.astype(BF16)

    def hand(name, dx, dy, device, part=None):
        ref = rows_t.at[group(dx, dy, 0)]
        if part is not None:
            ref = ref.at[pl.ds(part * width // 2, width // 2)]
        send("b" + name, ref, ref, device)

    def to_partner(dx, dy):
        hand(f"c{PLACES.index((dx, dy))}", dx, dy, partner)

    hand("x+", 0, 0, right)
    hand("x-", 0, 0, left)
    hand("y", 0, 0, beside)
    to_partner(0, 0)
    act_ref[...] = (pre_act * sigmoid).astype(BF16)
    arrived("bx+")
    hand("h+", 3, 0, right, 0)
    arrived("bx-")
    hand("h-", 1, 0, left, 1)
    arrived("by")
    hand("n+", 0, 1, right)
    hand("n-", 0, 1, left)
    for place_at in ((3, 0), (1, 0), (0, 1)):
        to_partner(*place_at)
    arrived("bh+")
    arrived("bh-")
    hand("y2", 2, 0, beside)
    to_partner(2, 0)
    arrived("bn+")
    to_partner(3, 1)
    arrived("bn-")
    to_partner(1, 1)
    arrived("by2")
    to_partner(2, 1)
    for j in range(8):
        arrived(f"bc{j}")

    def column_sums(b1, b2):
        left_side = jnp.concatenate([rows_t[k] for k in range(rows_t.shape[0])], axis=1)
        sums = dot(left_side, jnp.concatenate([slab[b1], slab[b2]], axis=1))
        for b, part in ((b1, sums[:, :tile]), (b2, sums[:, tile:])):
            totals[b] = part
            totals_low[b] = part.astype(BF16)

    where = {name: i for i, name in enumerate(REDUCE)}
    ways = (("m", -1, down, 0), ("p", 1, up, 1))
    middle = width // 2

    def leaf_half(way, kind, p, h, device):
        name = way + kind
        i = ("m", "p").index(way) * 2 + ("w4", "o4").index(kind)
        src = totals_low.at[block(p, 4), pl.ds(h * middle, middle)]
        send("r" + name, src, half_r.at[i], device)

    def leaf(name, p, d, device):
        send("r" + name, totals_low.at[block(p, d)], land_r.at[where[name]], device)

    def join_half(name, kind, p, d, way, h, device):
        arrived("r" + way + kind)
        i = ("m", "p").index(way) * 2 + ("w4", "o4").index(kind)
        b, slot = block(p, d), where[name]
        mid, rest = pl.ds(h * middle, middle), pl.ds((1 - h) * middle, middle)
        stage_r[slot, mid] = (totals[b, mid] + half_r[i].astype(F32)).astype(BF16)
        stage_r[slot, rest] = totals_low[b, rest]
        send("r" + name, stage_r.at[slot], land_r.at[slot], device)

    def join(name, children, p, d, device):
        value = totals[block(p, d)]
        for child in children:
            arrived("r" + child)
            value = value + land_r[where[child]].astype(F32)
        slot = where[name]
        stage_r[slot] = value.astype(BF16)
        send("r" + name, stage_r.at[slot], land_r.at[slot], device)

    column_sums(block(0, 4), block(1, 4))
    for way, s, device, h in ways:
        leaf_half(way, "o4", 1, h, device)
        leaf_half(way, "w4", 0, h, device)
    column_sums(block(1, 1), block(1, -1))
    for way, s, device, h in ways:
        leaf(way + "y1", 1, s, over)
    column_sums(block(1, 3), block(1, -3))
    for way, s, device, h in ways:
        join_half(way + "o3", "o4", 1, 3 * s, way, h, device)
    column_sums(block(0, 3), block(0, -3))
    for way, s, device, h in ways:
        join_half(way + "w3", "w4", 0, 3 * s, way, h, device)
    column_sums(block(1, 2), block(1, -2))
    for way, s, device, h in ways:
        join(way + "y2", [way + "o3"], 1, 2 * s, over)
    column_sums(block(1, 0), own)
    leaf("y0", 1, 0, over)
    column_sums(block(0, 2), block(0, -2))
    for way, s, device, h in ways:
        join(way + "w2", [way + "w3", way + "y2"], 0, 2 * s, device)
    column_sums(block(0, 1), block(0, -1))
    for way, s, device, h in ways:
        join(way + "w1", [way + "w2", way + "y1"], 0, s, device)

    blocks = range(panel.shape[0])
    slim = width // 16
    grad_low = pre_grad_t.astype(BF16)
    for i in range(width // tile):
        columns = slice(i * tile, (i + 1) * tile)
        term = dot(
            jnp.concatenate([totals_low[b] for b in blocks] + [grad_low], axis=1),
            jnp.concatenate(
                [panel[b, :, columns] for b in blocks] + [panel[own][:, columns]], axis=0
            ),
        ).T
        wown[columns] = term
        for j in range(tile // slim):
            wsend[i * (tile // slim) + j] = term[j * slim : (j + 1) * slim].astype(BF16)
    wcopies = []
    for i in range(1, 16):
        to = lax.rem(c + i, 16)
        copy = pltpu.make_async_remote_copy(
            wsend.at[to], wland.at[i], wsend_sem.at[i], wrecv_sem.at[i], device_id=(to, r)
        )
        copy.start()
        wcopies.append(copy)
    total = wown[pl.ds(pl.multiple_of(c * slim, slim), slim)]
    for i, copy in enumerate(wcopies):
        copy.wait_recv()
        total = total + wland[i + 1].astype(F32)
    two = slim // 16
    for i in range(16):
        wsend2[i, 0:two] = total[i * two : (i + 1) * two]
    wcopies2 = []
    for i in range(1, 16):
        to = lax.rem(r + i, 16)
        copy = pltpu.make_async_remote_copy(
            wsend2.at[to], wland2.at[i], wsend_sem.at[16 + i], wrecv_sem.at[16 + i],
            device_id=(c, to),
        )
        copy.start()
        wcopies2.append(copy)

    back_t = totals[own] + pre_grad_t
    for name in ("mw1", "pw1", "y0"):
        arrived("r" + name)
        back_t = back_t + land_r[where[name]].astype(F32)
    back = back_t.T.astype(BF16)
    input_rows = lax.dot_general(
        back, w_ref[...], (((1,), (1,)), ((), ())), preferred_element_type=F32
    ).astype(BF16)
    fgrad_ref[...] = dot(place.astype(BF16), input_rows).astype(BF16)

    pair = wsend2[r][0:two]
    for i, copy in enumerate(wcopies2):
        copy.wait_recv()
        pair = pair + wland2[i + 1][0:two]
    wgrad_ref[...] = pair * (1.0 / math.sqrt(tile * 256))
    for copy in [*copies.values(), *wcopies, *wcopies2]:
        copy.wait_send()


def on_device(features, reorder, weight, adjacency, tile_block, live_counts, grad_out):
    tile, width = features.shape
    slab, degree = dense_slab(tile_block[0, 0], live_counts[0, 0], adjacency)
    vmem = pl.BlockSpec(memory_space=pltpu.VMEM)
    rows = slab.shape[1]
    return pl.pallas_call(
        layer_kernel,
        in_specs=[vmem, vmem, vmem, pl.BlockSpec(memory_space=pl.ANY), vmem, vmem],
        out_specs=[vmem, vmem, vmem],
        out_shape=[
            jax.ShapeDtypeStruct((tile, width), BF16),
            jax.ShapeDtypeStruct((width // 256, width), F32),
            jax.ShapeDtypeStruct((tile, width), BF16),
        ],
        scratch_shapes=[
            pltpu.VMEM(slab.shape, BF16),
            pltpu.VMEM((16, tile, width), BF16),
            pltpu.VMEM((16, tile, width), BF16),
            pltpu.VMEM((rows, width), F32),
            pltpu.VMEM((len(FORWARD), tile + 16, width), BF16),
            pltpu.VMEM((len(FORWARD), tile + 16, width), BF16),
            pltpu.VMEM((16, width, tile), BF16),
            pltpu.VMEM((16, width, tile), F32),
            pltpu.VMEM((16, width, tile), BF16),
            pltpu.VMEM((len(REDUCE), width, tile), BF16),
            pltpu.VMEM((len(REDUCE), width, tile), BF16),
            pltpu.VMEM((4, width // 2, tile), BF16),
            pltpu.VMEM((16, width // 16, width), BF16),
            pltpu.VMEM((16, width // 16, width), BF16),
            pltpu.VMEM((width, width), F32),
            pltpu.VMEM((16, 8, width), F32),
            pltpu.VMEM((16, 8, width), F32),
            pltpu.SemaphoreType.DMA,
            pltpu.SemaphoreType.DMA((N_SEMS,)),
            pltpu.SemaphoreType.DMA((N_SEMS,)),
            pltpu.SemaphoreType.DMA((32,)),
            pltpu.SemaphoreType.DMA((32,)),
        ],
        compiler_params=pltpu.CompilerParams(
            collective_id=0, has_side_effects=True, vmem_limit_bytes=56 * 2**20
        ),
    )(features, reorder, weight, slab, degree, grad_out)


def solution(mesh):
    nodes = P(("col", "rep"), None)
    return jax.shard_map(
        on_device,
        mesh=mesh,
        in_specs=(
            nodes,
            nodes,
            P(),
            P("col", "rep", None, None, None, None),
            P("col", "rep", None, None),
            P("col", "rep", None),
            nodes,
        ),
        out_specs=(nodes, nodes, nodes),
        check_vma=False,
    )
```

```python
import math

import jax
import jax.numpy as jnp
from jax import lax
from jax.experimental import pallas as pl
from jax.experimental.pallas import tpu as pltpu
from jax.sharding import PartitionSpec as P

F32, BF16 = jnp.float32, jnp.bfloat16


def dot(a, b):
    return jnp.dot(a, b, preferred_element_type=F32)


OVER_REP = ["y00", "y01"] + [
    d + n
    for d in "pm"
    for n in ("w10", "w11", "w20", "w21", "w30", "w31", "w4", "o20", "o21", "o30", "o31", "o4", "y10", "y11")
]
FORWARD = [f"c{j}" for j in range(8)] + [
    n for m in ("a", "b+", "b-", "k", "d", "e+", "e-") for n in (m + "0", m + "1")
]
BACK = [f"c{j}" for j in range(8)] + [
    n for m in ("x+", "x-", "y", "h", "t", "n+", "n-") for n in (m + "0", m + "1")
]
SETS = [("g", OVER_REP), ("f", FORWARD), ("b", BACK), ("r", OVER_REP)]
INDEX = {n: i for i, n in enumerate(s + n for s, names in SETS for n in names)}
N_SEMS = len(INDEX)
SLOTS = {n: i for i, n in enumerate([f"c{j}" for j in range(8)] + ["a", "b+", "b-", "k", "d", "e+", "e-"])}
PIECES = {n: i for i, n in enumerate(["y0"] + [d + n for d in "pm" for n in ("w1", "w2", "w3", "w4", "o2", "o3", "o4", "y1")])}
PLACES = [(2, 1), (1, 1), (3, 1), (1, 0), (3, 0), (2, 0), (0, 1), (0, 0)]


def layer_kernel(
    feat_ref, order_ref, w_ref, tiles_hbm, block_ref, count_ref, grad_ref,
    act_ref, wgrad_ref, fgrad_ref,
    tiles, slab, ids, degrees, panel, projected, acc, stage_f, land_f, rows_t, totals, totals_low,
    stage_r, land_r, wsend, wland, wown, wsend2, wland2,
    tile_sem, send_sem, recv_sem, wsend_sem, wrecv_sem,
):
    tile, width = feat_ref.shape
    n_rows, n_slots = tiles.shape[:2]
    c, r = lax.axis_index("col"), lax.axis_index("rep")
    x, yl, core = c // 4, (c // 2) % 2, c % 2
    yh, z = r // 8, r % 8

    def group(dx, dy, dc):
        return ((x + dx) % 4) * 4 + ((yl + dy) % 2) * 2 + (core + dc) % 2

    def block(p, d):
        return ((yh + p) % 2) * 8 + (z + d + 8) % 8

    up, down, over = (c, block(0, 1)), (c, block(0, -1)), (c, block(1, 0))
    right, left, beside = (group(1, 0, 0), r), (group(3, 0, 0), r), (group(0, 1, 0), r)
    partner = (group(0, 0, 1), r)

    def fetch(k):
        return pltpu.make_async_copy(tiles_hbm.at[0, 0, k], tiles.at[k], tile_sem.at[k])

    barrier = pltpu.get_barrier_semaphore()
    for device in (up, down, over, right, left, beside, partner):
        pl.semaphore_signal(barrier, 1, device_id=device)

    @pl.loop(0, n_rows)
    def _(k):
        fetch(k).start()

    def iota(shape, dim):
        return lax.broadcasted_iota(jnp.int32, shape, dim)

    place = (iota((tile, tile), 0) == order_ref[...]).astype(F32)
    own = block(0, 0)
    panel[own] = dot(place.T.astype(BF16), feat_ref[...]).astype(BF16)

    n_blocks, strip = slab.shape[0], 16
    wide = n_slots * strip
    spread = (iota((n_slots, wide), 1) // strip == iota((n_slots, wide), 0)).astype(BF16)
    ids[...] = dot(block_ref[0, 0].astype(F32).astype(BF16), spread)

    def build(k):
        fetch(k).wait()
        shape = (n_blocks * strip + strip, wide)
        out_at, in_at = iota(shape, 0), iota(shape, 1)
        picked = (ids[pl.ds(k, 1), :] == (out_at // strip).astype(F32)) | (out_at >= n_blocks * strip)
        live = in_at // strip < count_ref[0, 0, k]
        pick = picked & live & (out_at % strip == in_at % strip)
        pick = jnp.where(pick, 1.0, 0.0).astype(BF16)
        slots = jnp.concatenate(
            [tiles[k, :, g * strip : (g + 1) * strip, :].reshape(wide, tile) for g in range(tile // strip)],
            axis=1,
        )
        out = dot(pick, slots)

        def rows_of(b):
            part = out[b * strip : (b + 1) * strip]
            return jnp.concatenate(
                [part[:, g * tile : (g + 1) * tile] for g in range(tile // strip)], axis=0
            )

        rows = pl.ds(pl.multiple_of(k * tile, tile), tile)
        for b in range(n_blocks):
            slab[b, rows] = rows_of(b).astype(BF16)
        degrees[k] = jnp.broadcast_to(
            jnp.sum(rows_of(n_blocks).T, axis=0, keepdims=True), degrees.shape[1:]
        )

    pl.loop(0, n_rows // 2)(build)
    pl.semaphore_wait(barrier, 7)
    copies = {}

    def send(name, src, dst, device):
        i = INDEX[name]
        copy = pltpu.make_async_remote_copy(
            src, dst, send_sem.at[i], recv_sem.at[i], device_id=device
        )
        copy.start()
        copies[name] = copy

    def arrived(name):
        copies[name].wait_recv()

    half = tile // 2

    def pass_on(name, p, d, device, h):
        ref = panel.at[block(p, d), pl.ds(h * half, half)]
        send("g" + name, ref, ref, device)

    def consume(b1, b2, first=False):
        for b in (b1, b2):
            projected[b] = dot(panel[b], w_ref[...]).astype(BF16)
        pair = jnp.concatenate([projected[b1], projected[b2]], axis=0)

        @pl.loop(0, slab.shape[1] // 512)
        def _(i):
            rows = pl.ds(pl.multiple_of(i * 512, 512), 512)
            part = dot(jnp.concatenate([slab[b1, rows], slab[b2, rows]], axis=1), pair)
            acc[rows] = part if first else acc[rows] + part

    ways = (("p", -1, up, 0), ("m", 1, down, 1))
    for h in (0, 1):
        for way, s, device, _ in ways:
            pass_on(f"{way}w1{h}", 0, 0, device, h)
        pass_on(f"y0{h}", 0, 0, over, h)
    pl.loop(n_rows // 2, n_rows)(build)
    for h in (0, 1):
        for way, s, device, _ in ways:
            arrived(f"g{way}w1{h}")
            pass_on(f"{way}w2{h}", 0, s, device, h)
            pass_on(f"{way}y1{h}", 0, s, over, h)
    for h in (0, 1):
        arrived(f"gy0{h}")
    consume(own, block(1, 0), first=True)
    for h in (0, 1):
        for way, s, device, _ in ways:
            arrived(f"g{way}w2{h}")
            pass_on(f"{way}w3{h}", 0, 2 * s, device, h)
    consume(block(0, 1), block(0, -1))
    for h in (0, 1):
        for way, s, device, _ in ways:
            arrived(f"g{way}y1{h}")
            pass_on(f"{way}o2{h}", 1, s, device, h)
    consume(block(0, 2), block(0, -2))
    for way, s, device, e in ways:
        arrived(f"g{way}w3{e}")
        pass_on(f"{way}w4", 0, 3 * s, device, e)
    consume(block(1, 1), block(1, -1))
    for h in (0, 1):
        for way, s, device, e in ways:
            arrived(f"g{way}o2{(h + e) % 2}")
            pass_on(f"{way}o3{(h + e) % 2}", 1, 2 * s, device, (h + e) % 2)
    for way, s, device, e in ways:
        arrived(f"g{way}w3{1 - e}")
    consume(block(0, 3), block(0, -3))
    for way, s, device, e in ways:
        arrived(f"g{way}o3{e}")
        pass_on(f"{way}o4", 1, 3 * s, device, e)
    consume(block(1, 2), block(1, -2))
    for way, s, device, e in ways:
        arrived(f"g{way}o3{1 - e}")
        arrived(f"g{way}w4")
    consume(block(1, 3), block(1, -3))
    for way, s, device, e in ways:
        arrived(f"g{way}o4")
    consume(block(0, 4), block(1, 4))

    def span(h):
        return slice(h * half, tile + 16 * h if h else half)

    def mine(dx, dy, dc, h):
        k = group(dx, dy, dc)
        rows = acc[pl.ds(pl.multiple_of(k * tile + h * half, half), half)]
        return rows, degrees[k][0:1]

    def pack(name, h, value):
        slot, (rows, degree) = SLOTS[name], value
        stage_f[slot, h * half : (h + 1) * half] = rows.astype(BF16)
        if h:
            high = degree.astype(BF16)
            low = (degree - high.astype(F32)).astype(BF16)
            none = jnp.zeros_like(high)
            stage_f[slot, tile : tile + 16] = jnp.concatenate(
                [jnp.broadcast_to(part, (16, tile)) for part in (high, low, none, none)], axis=1
            )

    def plus(value, name, h):
        slot, (rows, degree) = SLOTS[name], value
        rows = rows + land_f[slot, h * half : (h + 1) * half].astype(F32)
        if h:
            tail = land_f[slot, tile : tile + 16].astype(F32)
            degree = degree + tail[0:1, 0:tile] + tail[0:1, tile : 2 * tile]
        return rows, degree

    def ship(name, h, device):
        slot = SLOTS[name]
        at = pl.ds(span(h).start, span(h).stop - span(h).start)
        send(f"f{name}{h}", stage_f.at[slot, at], land_f.at[slot, at], device)

    for j, (dx, dy) in enumerate(PLACES):
        for h in (0, 1):
            pack(f"c{j}", h, mine(dx, dy, 1, h))
        send(f"fc{j}", stage_f.at[j], land_f.at[j], partner)

    def both(dx, dy, h):
        return plus(mine(dx, dy, 0, h), f"c{PLACES.index((dx, dy))}", h)

    def go(name, h, value, device):
        pack(name, h, value)
        ship(name, h, device)

    sides = (("+", 1, right, 0), ("-", 3, left, 1))
    arrived("fc0")
    for h in (0, 1):
        go("a", h, both(2, 1, h), beside)
    for j, (s, dx, device, e) in enumerate(sides):
        arrived(f"fc{1 + j}")
        go("b" + s, e, both(dx, 1, e), device)
        go("b" + s, 1 - e, both(dx, 1, 1 - e), device)
    for j, (s, dx, device, e) in enumerate(sides):
        arrived(f"fc{3 + j}")
        go("e" + s, 1 - e, both(dx, 0, 1 - e), device)
    arrived("fc5")
    for s, dx, device, e in sides:
        arrived(f"fa{e}")
        go("k", e, plus(both(2, 0, e), "a", e), device)
    arrived("fc6")
    for h in (0, 1):
        arrived(f"fb+{h}")
        arrived(f"fb-{h}")
        go("d", h, plus(plus(both(0, 1, h), "b+", h), "b-", h), beside)
    for s, dx, device, e in sides:
        arrived(f"fk{e}")
        go("e" + s, e, plus(both(dx, 0, e), "k", e), device)
    arrived("fc7")
    parts = []
    for h in (0, 1):
        value = both(0, 0, h)
        for name in ("d", "e+", "e-"):
            arrived(f"f{name}{h}")
            value = plus(value, name, h)
        parts.append(value)
    summed = jnp.concatenate([parts[0][0], parts[1][0]], axis=0)
    degree = parts[1][1]

    scale = lax.rsqrt(1.0 + jnp.broadcast_to(degree, (tile, tile)).T)
    scale = jnp.concatenate([scale] * (width // tile), axis=1)
    pre_act = summed * scale + projected[own].astype(F32)
    sigmoid = 1.0 / (1.0 + jnp.exp(-pre_act))
    pre_grad = grad_ref[...].astype(F32) * sigmoid * (1.0 + pre_act * (1.0 - sigmoid))
    rows_t[c] = (pre_grad * scale).T.astype(BF16)

    middle = width // 2

    def hand(name, dx, dy, device, h):
        ref = rows_t.at[group(dx, dy, 0), pl.ds(h * middle, middle)]
        send("b" + name, ref, ref, device)

    def to_partner(dx, dy):
        ref = rows_t.at[group(dx, dy, 0)]
        send(f"bc{PLACES.index((dx, dy))}", ref, ref, partner)

    for h in (0, 1):
        for s, dx, device, e in sides:
            hand(f"x{s}{(h + e) % 2}", 0, 0, device, (h + e) % 2)
        hand(f"y{h}", 0, 0, beside, h)
    to_partner(0, 0)
    pre_grad_t = pre_grad.T
    act_ref[...] = (pre_act * sigmoid).astype(BF16)
    for s, dx, device, e in sides:
        arrived(f"bx{s}{e}")
        hand(f"h{e}", 4 - dx, 0, device, e)
    for h in (0, 1):
        arrived(f"by{h}")
        for s, dx, device, e in sides:
            hand(f"n{s}{h}", 0, 1, device, h)
    for s, dx, device, e in sides:
        arrived(f"bx{s}{1 - e}")
        to_partner(4 - dx, 0)
    to_partner(0, 1)
    for e in (0, 1):
        arrived(f"bh{e}")
        hand(f"t{e}", 2, 0, beside, e)
    to_partner(2, 0)
    for s, dx, device, e in sides:
        arrived(f"bn{s}0")
        arrived(f"bn{s}1")
        to_partner(4 - dx, 1)
    arrived("bt0")
    arrived("bt1")
    to_partner(2, 1)
    for j in range(8):
        arrived(f"bc{j}")

    def column_sums(b1, b2):
        left_side = jnp.concatenate([rows_t[k] for k in range(rows_t.shape[0])], axis=1)
        sums = dot(left_side, jnp.concatenate([slab[b1], slab[b2]], axis=1))
        for b, part in ((b1, sums[:, :tile]), (b2, sums[:, tile:])):
            totals[b] = part
            totals_low[b] = part.astype(BF16)

    ways = (("m", -1, down, 0), ("p", 1, up, 1))

    def leaf(name, h, p, d, device, one=False):
        at = pl.ds(h * middle, middle)
        src, dst = totals_low.at[block(p, d), at], land_r.at[PIECES[name], at]
        send(f"r{name}" if one else f"r{name}{h}", src, dst, device)

    def join(name, children, h, p, d, device):
        at, slot = pl.ds(h * middle, middle), PIECES[name]
        value = totals[block(p, d), at]
        for child in children:
            arrived(f"r{child}" if child[1:] in ("w4", "o4") else f"r{child}{h}")
            value = value + land_r[PIECES[child], at].astype(F32)
        stage_r[slot, at] = value.astype(BF16)
        send(f"r{name}{h}", stage_r.at[slot, at], land_r.at[slot, at], device)

    column_sums(block(0, 4), block(1, 4))
    for way, s, device, e in ways:
        leaf(way + "o4", e, 1, 4, device, one=True)
    for way, s, device, e in ways:
        leaf(way + "w4", e, 0, 4, device, one=True)
    column_sums(block(1, 3), block(1, -3))
    for way, s, device, e in ways:
        leaf(way + "o3", 1 - e, 1, 3 * s, device)
    column_sums(block(0, 3), block(0, -3))
    for way, s, device, e in ways:
        leaf(way + "w3", 1 - e, 0, 3 * s, device)
    column_sums(block(1, 2), block(1, -2))
    column_sums(block(1, 0), own)
    for h in (0, 1):
        leaf("y0", h, 1, 0, over)
    for way, s, device, e in ways:
        join(way + "o3", [way + "o4"], e, 1, 3 * s, device)
    for way, s, device, e in ways:
        join(way + "w3", [way + "w4"], e, 0, 3 * s, device)
    for way, s, device, e in ways:
        join(way + "o2", [way + "o3"], 1 - e, 1, 2 * s, device)
    column_sums(block(1, 1), block(1, -1))
    column_sums(block(0, 2), block(0, -2))
    for way, s, device, e in ways:
        join(way + "o2", [way + "o3"], e, 1, 2 * s, device)
    for way, s, device, e in ways:
        join(way + "w2", [way + "w3"], 1 - e, 0, 2 * s, device)
    column_sums(block(0, 1), block(0, -1))
    for way, s, device, e in ways:
        join(way + "y1", [way + "o2"], 1 - e, 1, s, over)
    for way, s, device, e in ways:
        join(way + "w2", [way + "w3"], e, 0, 2 * s, device)
    for way, s, device, e in ways:
        join(way + "y1", [way + "o2"], e, 1, s, over)

    blocks = range(panel.shape[0])
    slim = width // 16
    grad_low = pre_grad_t.astype(BF16)
    for i in range(width // tile):
        columns = slice(i * tile, (i + 1) * tile)
        term = dot(
            jnp.concatenate([totals_low[b] for b in blocks] + [grad_low], axis=1),
            jnp.concatenate(
                [panel[b, :, columns] for b in blocks] + [panel[own][:, columns]], axis=0
            ),
        ).T
        wown[columns] = term
        for j in range(tile // slim):
            wsend[i * (tile // slim) + j] = term[j * slim : (j + 1) * slim].astype(BF16)
    wcopies = []
    for i in range(1, 16):
        to = lax.rem(c + i, 16)
        copy = pltpu.make_async_remote_copy(
            wsend.at[to], wland.at[i], wsend_sem.at[i], wrecv_sem.at[i], device_id=(to, r)
        )
        copy.start()
        wcopies.append(copy)
    for way, s, device, e in ways:
        join(way + "w1", [way + "w2", way + "y1"], 1 - e, 0, s, device)
    total = wown[pl.ds(pl.multiple_of(c * slim, slim), slim)]
    for i, copy in enumerate(wcopies):
        copy.wait_recv()
        total = total + wland[i + 1].astype(F32)
    two, lanes = slim // 16, tile
    for i in range(16):
        rows = total[i * two : (i + 1) * two]
        wsend2[i] = jnp.concatenate(
            [rows[:, q * lanes : (q + 1) * lanes] for q in range(width // lanes)], axis=0
        )
    wcopies2 = []
    for i in range(1, 16):
        to = lax.rem(r + i, 16)
        copy = pltpu.make_async_remote_copy(
            wsend2.at[to], wland2.at[i], wsend_sem.at[16 + i], wrecv_sem.at[16 + i],
            device_id=(c, to),
        )
        copy.start()
        wcopies2.append(copy)
    for way, s, device, e in ways:
        join(way + "w1", [way + "w2", way + "y1"], e, 0, s, device)

    back = []
    for h in (0, 1):
        at = pl.ds(h * middle, middle)
        value = totals[own, at] + pre_grad_t[h * middle : (h + 1) * middle]
        for name in ("y0", "mw1", "pw1"):
            arrived(f"r{name}{h}")
            value = value + land_r[PIECES[name], at].astype(F32)
        back.append(value)
    back = jnp.concatenate(back, axis=0).T.astype(BF16)
    input_rows = lax.dot_general(
        back, w_ref[...], (((1,), (1,)), ((), ())), preferred_element_type=F32
    ).astype(BF16)
    fgrad_ref[...] = dot(place.astype(BF16), input_rows).astype(BF16)

    pair = wsend2[r]
    for i, copy in enumerate(wcopies2):
        copy.wait_recv()
        pair = pair + wland2[i + 1]
    pair = jnp.concatenate([pair[q * two : (q + 1) * two] for q in range(width // lanes)], axis=1)
    wgrad_ref[...] = pair * (1.0 / math.sqrt(tile * 256))
    for copy in [*copies.values(), *wcopies, *wcopies2]:
        copy.wait_send()


def on_device(features, reorder, weight, adjacency, tile_block, live_counts, grad_out):
    tile, width = features.shape
    _, _, rows, slots, _, _ = adjacency.shape
    blocks = 16
    vmem = pl.BlockSpec(memory_space=pltpu.VMEM)
    return pl.pallas_call(
        layer_kernel,
        in_specs=[
            vmem, vmem, vmem, pl.BlockSpec(memory_space=pl.ANY), vmem,
            pl.BlockSpec(memory_space=pltpu.SMEM), vmem,
        ],
        out_specs=[vmem, vmem, vmem],
        out_shape=[
            jax.ShapeDtypeStruct((tile, width), BF16),
            jax.ShapeDtypeStruct((width // 256, width), F32),
            jax.ShapeDtypeStruct((tile, width), BF16),
        ],
        scratch_shapes=[
            pltpu.VMEM((rows, slots, tile, tile), BF16),
            pltpu.VMEM((blocks, rows * tile, tile), BF16),
            pltpu.VMEM((rows, slots * 16), F32),
            pltpu.VMEM((rows, 8, tile), F32),
            pltpu.VMEM((blocks, tile, width), BF16),
            pltpu.VMEM((blocks, tile, width), BF16),
            pltpu.VMEM((rows * tile, width), F32),
            pltpu.VMEM((len(SLOTS), tile + 16, width), BF16),
            pltpu.VMEM((len(SLOTS), tile + 16, width), BF16),
            pltpu.VMEM((16, width, tile), BF16),
            pltpu.VMEM((16, width, tile), F32),
            pltpu.VMEM((16, width, tile), BF16),
            pltpu.VMEM((len(PIECES), width, tile), BF16),
            pltpu.VMEM((len(PIECES), width, tile), BF16),
            pltpu.VMEM((16, width // 16, width), BF16),
            pltpu.VMEM((16, width // 16, width), BF16),
            pltpu.VMEM((width, width), F32),
            pltpu.VMEM((16, 8, tile), F32),
            pltpu.VMEM((16, 8, tile), F32),
            pltpu.SemaphoreType.DMA((rows,)),
            pltpu.SemaphoreType.DMA((N_SEMS,)),
            pltpu.SemaphoreType.DMA((N_SEMS,)),
            pltpu.SemaphoreType.DMA((32,)),
            pltpu.SemaphoreType.DMA((32,)),
        ],
        compiler_params=pltpu.CompilerParams(
            collective_id=0, has_side_effects=True, vmem_limit_bytes=60 * 2**20
        ),
    )(features, reorder, weight, adjacency, tile_block, live_counts, grad_out)


def solution(mesh):
    nodes = P(("col", "rep"), None)
    return jax.shard_map(
        on_device,
        mesh=mesh,
        in_specs=(
            nodes,
            nodes,
            P(),
            P("col", "rep", None, None, None, None),
            P("col", "rep", None, None),
            P("col", "rep", None),
            nodes,
        ),
        out_specs=(nodes, nodes, nodes),
        check_vma=False,
    )
```

```python
import math

import jax
import jax.numpy as jnp
from jax import lax
from jax.experimental import pallas as pl
from jax.experimental.pallas import tpu as pltpu
from jax.sharding import PartitionSpec as P

F32, BF16 = jnp.float32, jnp.bfloat16


def dot(a, b):
    return jnp.dot(a, b, preferred_element_type=F32)


OVER_REP = ["y00", "y01"] + [
    d + n
    for d in "pm"
    for n in ("w10", "w11", "w20", "w21", "w30", "w31", "w4", "o20", "o21", "o30", "o31", "o4", "y10", "y11")
]
FORWARD = [f"c{j}" for j in range(8)] + [
    n for m in ("a", "b+", "b-", "k", "d", "e+", "e-") for n in (m + "0", m + "1")
]
BACK = [f"c{j}" for j in range(8)] + [
    n for m in ("x+", "x-", "y", "h", "t", "n+", "n-") for n in (m + "0", m + "1")
]
SETS = [("g", OVER_REP), ("f", FORWARD), ("b", BACK), ("r", OVER_REP)]
INDEX = {n: i for i, n in enumerate(s + n for s, names in SETS for n in names)}
N_SEMS = len(INDEX)
SLOTS = {n: i for i, n in enumerate([f"c{j}" for j in range(8)] + ["a", "b+", "b-", "k", "d", "e+", "e-"])}
PIECES = {n: i for i, n in enumerate(["y0"] + [d + n for d in "pm" for n in ("w1", "w2", "w3", "w4", "o2", "o3", "o4", "y1")])}
PLACES = [(2, 1), (1, 1), (3, 1), (1, 0), (3, 0), (2, 0), (0, 1), (0, 0)]


def layer_kernel(
    feat_ref, order_ref, w_ref, tiles_hbm, block_ref, count_ref, grad_ref,
    act_ref, wgrad_ref, fgrad_ref,
    tiles, slab, ids, degrees, panel, projected, acc, stage_f, land_f, rows_t, totals, totals_low,
    stage_r, land_r, wown, wcore, wcore_in, wmid, wmid_low, wmid_in, wlast, wlast_low, wlast_in,
    wsend2, wland2,
    tile_sem, send_sem, recv_sem, wsend_sem, wrecv_sem,
):
    tile, width = feat_ref.shape
    n_rows, n_slots = tiles.shape[:2]
    c, r = lax.axis_index("col"), lax.axis_index("rep")
    x, yl, core = c // 4, (c // 2) % 2, c % 2
    yh, z = r // 8, r % 8

    def group(dx, dy, dc):
        return ((x + dx) % 4) * 4 + ((yl + dy) % 2) * 2 + (core + dc) % 2

    def block(p, d):
        return ((yh + p) % 2) * 8 + (z + d + 8) % 8

    up, down, over = (c, block(0, 1)), (c, block(0, -1)), (c, block(1, 0))
    right, left, beside = (group(1, 0, 0), r), (group(3, 0, 0), r), (group(0, 1, 0), r)
    partner = (group(0, 0, 1), r)

    def fetch(k):
        return pltpu.make_async_copy(tiles_hbm.at[0, 0, k], tiles.at[k], tile_sem.at[k])

    barrier = pltpu.get_barrier_semaphore()
    for device in (up, down, over, right, left, beside, partner):
        pl.semaphore_signal(barrier, 1, device_id=device)

    @pl.loop(0, n_rows)
    def _(k):
        fetch(k).start()

    def iota(shape, dim):
        return lax.broadcasted_iota(jnp.int32, shape, dim)

    place = (iota((tile, tile), 0) == order_ref[...]).astype(F32)
    own = block(0, 0)
    panel[own] = dot(place.T.astype(BF16), feat_ref[...]).astype(BF16)

    n_blocks, strip = slab.shape[0], 16
    wide = n_slots * strip
    spread = (iota((n_slots, wide), 1) // strip == iota((n_slots, wide), 0)).astype(BF16)
    ids[...] = dot(block_ref[0, 0].astype(F32).astype(BF16), spread)

    def build(k):
        fetch(k).wait()
        shape = (n_blocks * strip + strip, wide)
        out_at, in_at = iota(shape, 0), iota(shape, 1)
        picked = (ids[pl.ds(k, 1), :] == (out_at // strip).astype(F32)) | (out_at >= n_blocks * strip)
        live = in_at // strip < count_ref[0, 0, k]
        pick = picked & live & (out_at % strip == in_at % strip)
        pick = jnp.where(pick, 1.0, 0.0).astype(BF16)
        slots = jnp.concatenate(
            [tiles[k, :, g * strip : (g + 1) * strip, :].reshape(wide, tile) for g in range(tile // strip)],
            axis=1,
        )
        out = dot(pick, slots)

        def rows_of(b):
            part = out[b * strip : (b + 1) * strip]
            return jnp.concatenate(
                [part[:, g * tile : (g + 1) * tile] for g in range(tile // strip)], axis=0
            )

        rows = pl.ds(pl.multiple_of(k * tile, tile), tile)
        for b in range(n_blocks):
            slab[b, rows] = rows_of(b).astype(BF16)
        degrees[k] = jnp.broadcast_to(
            jnp.sum(rows_of(n_blocks).T, axis=0, keepdims=True), degrees.shape[1:]
        )

    pl.loop(0, n_rows // 2)(build)
    pl.semaphore_wait(barrier, 7)
    copies = {}

    def send(name, src, dst, device):
        i = INDEX[name]
        copy = pltpu.make_async_remote_copy(
            src, dst, send_sem.at[i], recv_sem.at[i], device_id=device
        )
        copy.start()
        copies[name] = copy

    def arrived(name):
        copies[name].wait_recv()

    half = tile // 2

    def pass_on(name, p, d, device, h):
        ref = panel.at[block(p, d), pl.ds(h * half, half)]
        send("g" + name, ref, ref, device)

    def consume(b1, b2, first=False):
        for b in (b1, b2):
            projected[b] = dot(panel[b], w_ref[...]).astype(BF16)
        pair = jnp.concatenate([projected[b1], projected[b2]], axis=0)

        @pl.loop(0, slab.shape[1] // 512)
        def _(i):
            rows = pl.ds(pl.multiple_of(i * 512, 512), 512)
            part = dot(jnp.concatenate([slab[b1, rows], slab[b2, rows]], axis=1), pair)
            acc[rows] = part if first else acc[rows] + part

    ways = (("p", -1, up, 0), ("m", 1, down, 1))
    for h in (0, 1):
        for way, s, device, _ in ways:
            pass_on(f"{way}w1{h}", 0, 0, device, h)
        pass_on(f"y0{h}", 0, 0, over, h)
    pl.loop(n_rows // 2, n_rows)(build)
    for h in (0, 1):
        for way, s, device, _ in ways:
            arrived(f"g{way}w1{h}")
            pass_on(f"{way}w2{h}", 0, s, device, h)
            pass_on(f"{way}y1{h}", 0, s, over, h)
    for h in (0, 1):
        arrived(f"gy0{h}")
    consume(own, block(1, 0), first=True)
    for h in (0, 1):
        for way, s, device, _ in ways:
            arrived(f"g{way}w2{h}")
            pass_on(f"{way}w3{h}", 0, 2 * s, device, h)
    consume(block(0, 1), block(0, -1))
    for h in (0, 1):
        for way, s, device, _ in ways:
            arrived(f"g{way}y1{h}")
            pass_on(f"{way}o2{h}", 1, s, device, h)
    consume(block(0, 2), block(0, -2))
    for way, s, device, e in ways:
        arrived(f"g{way}w3{e}")
        pass_on(f"{way}w4", 0, 3 * s, device, e)
    consume(block(1, 1), block(1, -1))
    for h in (0, 1):
        for way, s, device, e in ways:
            arrived(f"g{way}o2{(h + e) % 2}")
            pass_on(f"{way}o3{(h + e) % 2}", 1, 2 * s, device, (h + e) % 2)
    for way, s, device, e in ways:
        arrived(f"g{way}w3{1 - e}")
    consume(block(0, 3), block(0, -3))
    for way, s, device, e in ways:
        arrived(f"g{way}o3{e}")
        pass_on(f"{way}o4", 1, 3 * s, device, e)
    consume(block(1, 2), block(1, -2))
    for way, s, device, e in ways:
        arrived(f"g{way}o3{1 - e}")
        arrived(f"g{way}w4")
    consume(block(1, 3), block(1, -3))
    for way, s, device, e in ways:
        arrived(f"g{way}o4")
    consume(block(0, 4), block(1, 4))

    def span(h):
        return slice(h * half, tile + 16 * h if h else half)

    def mine(dx, dy, dc, h):
        k = group(dx, dy, dc)
        rows = acc[pl.ds(pl.multiple_of(k * tile + h * half, half), half)]
        return rows, degrees[k][0:1]

    def pack(name, h, value):
        slot, (rows, degree) = SLOTS[name], value
        stage_f[slot, h * half : (h + 1) * half] = rows.astype(BF16)
        if h:
            high = degree.astype(BF16)
            low = (degree - high.astype(F32)).astype(BF16)
            none = jnp.zeros_like(high)
            stage_f[slot, tile : tile + 16] = jnp.concatenate(
                [jnp.broadcast_to(part, (16, tile)) for part in (high, low, none, none)], axis=1
            )

    def plus(value, name, h):
        slot, (rows, degree) = SLOTS[name], value
        rows = rows + land_f[slot, h * half : (h + 1) * half].astype(F32)
        if h:
            tail = land_f[slot, tile : tile + 16].astype(F32)
            degree = degree + tail[0:1, 0:tile] + tail[0:1, tile : 2 * tile]
        return rows, degree

    def ship(name, h, device):
        slot = SLOTS[name]
        at = pl.ds(span(h).start, span(h).stop - span(h).start)
        send(f"f{name}{h}", stage_f.at[slot, at], land_f.at[slot, at], device)

    for j, (dx, dy) in enumerate(PLACES):
        for h in (0, 1):
            pack(f"c{j}", h, mine(dx, dy, 1, h))
        send(f"fc{j}", stage_f.at[j], land_f.at[j], partner)

    def both(dx, dy, h):
        return plus(mine(dx, dy, 0, h), f"c{PLACES.index((dx, dy))}", h)

    def go(name, h, value, device):
        pack(name, h, value)
        ship(name, h, device)

    sides = (("+", 1, right, 0), ("-", 3, left, 1))
    arrived("fc0")
    for h in (0, 1):
        go("a", h, both(2, 1, h), beside)
    for j, (s, dx, device, e) in enumerate(sides):
        arrived(f"fc{1 + j}")
        go("b" + s, e, both(dx, 1, e), device)
        go("b" + s, 1 - e, both(dx, 1, 1 - e), device)
    for j, (s, dx, device, e) in enumerate(sides):
        arrived(f"fc{3 + j}")
        go("e" + s, 1 - e, both(dx, 0, 1 - e), device)
    arrived("fc5")
    for s, dx, device, e in sides:
        arrived(f"fa{e}")
        go("k", e, plus(both(2, 0, e), "a", e), device)
    arrived("fc6")
    for h in (0, 1):
        arrived(f"fb+{h}")
        arrived(f"fb-{h}")
        go("d", h, plus(plus(both(0, 1, h), "b+", h), "b-", h), beside)
    for s, dx, device, e in sides:
        arrived(f"fk{e}")
        go("e" + s, e, plus(both(dx, 0, e), "k", e), device)
    arrived("fc7")
    parts = []
    for h in (0, 1):
        value = both(0, 0, h)
        for name in ("d", "e+", "e-"):
            arrived(f"f{name}{h}")
            value = plus(value, name, h)
        parts.append(value)
    summed = jnp.concatenate([parts[0][0], parts[1][0]], axis=0)
    degree = parts[1][1]

    scale = lax.rsqrt(1.0 + jnp.broadcast_to(degree, (tile, tile)).T)
    scale = jnp.concatenate([scale] * (width // tile), axis=1)
    pre_act = summed * scale + projected[own].astype(F32)
    sigmoid = 1.0 / (1.0 + jnp.exp(-pre_act))
    pre_grad = grad_ref[...].astype(F32) * sigmoid * (1.0 + pre_act * (1.0 - sigmoid))
    rows_t[c] = (pre_grad * scale).T.astype(BF16)

    middle = width // 2

    def hand(name, dx, dy, device, h):
        ref = rows_t.at[group(dx, dy, 0), pl.ds(h * middle, middle)]
        send("b" + name, ref, ref, device)

    def to_partner(dx, dy):
        ref = rows_t.at[group(dx, dy, 0)]
        send(f"bc{PLACES.index((dx, dy))}", ref, ref, partner)

    for h in (0, 1):
        for s, dx, device, e in sides:
            hand(f"x{s}{(h + e) % 2}", 0, 0, device, (h + e) % 2)
        hand(f"y{h}", 0, 0, beside, h)
    to_partner(0, 0)
    pre_grad_t = pre_grad.T
    act_ref[...] = (pre_act * sigmoid).astype(BF16)
    for s, dx, device, e in sides:
        arrived(f"bx{s}{e}")
        hand(f"h{e}", 4 - dx, 0, device, e)
    for h in (0, 1):
        arrived(f"by{h}")
        for s, dx, device, e in sides:
            hand(f"n{s}{h}", 0, 1, device, h)
    for s, dx, device, e in sides:
        arrived(f"bx{s}{1 - e}")
        to_partner(4 - dx, 0)
    to_partner(0, 1)
    for e in (0, 1):
        arrived(f"bh{e}")
        hand(f"t{e}", 2, 0, beside, e)
    to_partner(2, 0)
    for s, dx, device, e in sides:
        arrived(f"bn{s}0")
        arrived(f"bn{s}1")
        to_partner(4 - dx, 1)
    arrived("bt0")
    arrived("bt1")
    to_partner(2, 1)
    for j in range(8):
        arrived(f"bc{j}")

    def column_sums(b1, b2):
        left_side = jnp.concatenate([rows_t[k] for k in range(rows_t.shape[0])], axis=1)
        sums = dot(left_side, jnp.concatenate([slab[b1], slab[b2]], axis=1))
        for b, part in ((b1, sums[:, :tile]), (b2, sums[:, tile:])):
            totals[b] = part
            totals_low[b] = part.astype(BF16)

    ways = (("m", -1, down, 0), ("p", 1, up, 1))

    def leaf(name, h, p, d, device, one=False):
        at = pl.ds(h * middle, middle)
        src, dst = totals_low.at[block(p, d), at], land_r.at[PIECES[name], at]
        send(f"r{name}" if one else f"r{name}{h}", src, dst, device)

    def join(name, children, h, p, d, device):
        at, slot = pl.ds(h * middle, middle), PIECES[name]
        value = totals[block(p, d), at]
        for child in children:
            arrived(f"r{child}" if child[1:] in ("w4", "o4") else f"r{child}{h}")
            value = value + land_r[PIECES[child], at].astype(F32)
        stage_r[slot, at] = value.astype(BF16)
        send(f"r{name}{h}", stage_r.at[slot, at], land_r.at[slot, at], device)

    column_sums(block(0, 4), block(1, 4))
    for way, s, device, e in ways:
        leaf(way + "o4", e, 1, 4, device, one=True)
    for way, s, device, e in ways:
        leaf(way + "w4", e, 0, 4, device, one=True)
    column_sums(block(1, 3), block(1, -3))
    for way, s, device, e in ways:
        leaf(way + "o3", 1 - e, 1, 3 * s, device)
    column_sums(block(0, 3), block(0, -3))
    for way, s, device, e in ways:
        leaf(way + "w3", 1 - e, 0, 3 * s, device)
    column_sums(block(1, 0), own)
    for h in (0, 1):
        leaf("y0", h, 1, 0, over)
    column_sums(block(1, 2), block(1, -2))
    for way, s, device, e in ways:
        join(way + "o3", [way + "o4"], e, 1, 3 * s, device)
    for way, s, device, e in ways:
        join(way + "w3", [way + "w4"], e, 0, 3 * s, device)
    column_sums(block(1, 1), block(1, -1))
    for way, s, device, e in ways:
        join(way + "o2", [way + "o3"], 1 - e, 1, 2 * s, device)
    column_sums(block(0, 2), block(0, -2))
    column_sums(block(0, 1), block(0, -1))
    for way, s, device, e in ways:
        join(way + "o2", [way + "o3"], e, 1, 2 * s, device)
    for way, s, device, e in ways:
        join(way + "w2", [way + "w3"], 1 - e, 0, 2 * s, device)

    blocks = range(panel.shape[0])
    slim = width // 16
    grad_low = pre_grad_t.astype(BF16)
    wcopies = {}

    def wsend(name, i, src, dst, device):
        copy = pltpu.make_async_remote_copy(
            src, dst, wsend_sem.at[i], wrecv_sem.at[i], device_id=device
        )
        copy.start()
        wcopies[name] = copy

    for i in range(width // tile):
        columns = slice(i * tile, (i + 1) * tile)
        term = dot(
            jnp.concatenate([totals_low[b] for b in blocks] + [grad_low], axis=1),
            jnp.concatenate(
                [panel[b, :, columns] for b in blocks] + [panel[own][:, columns]], axis=0
            ),
        ).T
        wown[columns] = term
        for j in range(tile // slim):
            rows = term[j * slim : (j + 1) * slim].astype(BF16)
            wcore[j % 2, pl.ds((i * 2 + j // 2) * slim, slim)] = rows
    wsend("core", 0, wcore.at[1 - core], wcore_in, partner)

    for way, s, device, e in ways:
        join(way + "y1", [way + "o2"], 1 - e, 1, s, over)
    wcopies["core"].wait_recv()
    for i in range(4):
        for j in range(2):
            at = pl.ds((i * 2 + j) * slim, slim)
            rows = wown[pl.ds(pl.multiple_of((i * 4 + j * 2 + core) * slim, slim), slim)]
            rows = rows + wcore_in[at].astype(F32)
            wmid[i, pl.ds(j * slim, slim)] = rows
            wmid_low[i, pl.ds(j * slim, slim)] = rows.astype(BF16)
    for i in range(1, 4):
        wsend(f"x{i}", i, wmid_low.at[(x + i) % 4], wmid_in.at[i], (group(i, 0, 0), r))
    for way, s, device, e in ways:
        join(way + "w2", [way + "w3"], e, 0, 2 * s, device)
    for way, s, device, e in ways:
        join(way + "y1", [way + "o2"], e, 1, s, over)
    pair = wmid[x]
    for i in range(1, 4):
        wcopies[f"x{i}"].wait_recv()
        pair = pair + wmid_in[i].astype(F32)
    for j in range(2):
        wlast[j] = pair[j * slim : (j + 1) * slim]
        wlast_low[j] = pair[j * slim : (j + 1) * slim].astype(BF16)
    wsend("y", 4, wlast_low.at[1 - yl], wlast_in, beside)
    for way, s, device, e in ways:
        join(way + "w1", [way + "w2", way + "y1"], 1 - e, 0, s, device)
    wcopies["y"].wait_recv()
    total = wlast[yl] + wlast_in[...].astype(F32)
    two, lanes = slim // 16, tile
    for i in range(16):
        rows = total[i * two : (i + 1) * two]
        wsend2[i] = jnp.concatenate(
            [rows[:, q * lanes : (q + 1) * lanes] for q in range(width // lanes)], axis=0
        )
    for i in range(1, 16):
        to = lax.rem(r + i, 16)
        wsend(f"r{i}", 16 + i, wsend2.at[to], wland2.at[i], (c, to))
    for way, s, device, e in ways:
        join(way + "w1", [way + "w2", way + "y1"], e, 0, s, device)

    back = []
    for h in (0, 1):
        at = pl.ds(h * middle, middle)
        value = totals[own, at] + pre_grad_t[h * middle : (h + 1) * middle]
        for name in ("y0", "mw1", "pw1"):
            arrived(f"r{name}{h}")
            value = value + land_r[PIECES[name], at].astype(F32)
        back.append(value)
    back = jnp.concatenate(back, axis=0).T.astype(BF16)
    input_rows = lax.dot_general(
        back, w_ref[...], (((1,), (1,)), ((), ())), preferred_element_type=F32
    ).astype(BF16)
    fgrad_ref[...] = dot(place.astype(BF16), input_rows).astype(BF16)

    pair = wsend2[r]
    for i in range(1, 16):
        wcopies[f"r{i}"].wait_recv()
        pair = pair + wland2[i]
    pair = jnp.concatenate([pair[q * two : (q + 1) * two] for q in range(width // lanes)], axis=1)
    wgrad_ref[...] = pair * (1.0 / math.sqrt(tile * 256))
    for copy in [*copies.values(), *wcopies.values()]:
        copy.wait_send()


def place_kernel(*refs):
    for src, dst in zip(refs[: len(refs) // 2], refs[len(refs) // 2 :], strict=True):
        dst[...] = src[...]


def on_device(features, reorder, weight, adjacency, tile_block, live_counts, grad_out):
    tile, width = features.shape
    _, _, rows, slots, _, _ = adjacency.shape
    blocks = 16
    vmem = pl.BlockSpec(memory_space=pltpu.VMEM)
    results = pl.pallas_call(
        layer_kernel,
        in_specs=[
            vmem, vmem, vmem, pl.BlockSpec(memory_space=pl.ANY), vmem,
            pl.BlockSpec(memory_space=pltpu.SMEM), vmem,
        ],
        out_specs=[vmem, vmem, vmem],
        out_shape=[
            jax.ShapeDtypeStruct((tile, width), BF16),
            jax.ShapeDtypeStruct((width // 256, width), F32),
            jax.ShapeDtypeStruct((tile, width), BF16),
        ],
        scratch_shapes=[
            pltpu.VMEM((rows, slots, tile, tile), BF16),
            pltpu.VMEM((blocks, rows * tile, tile), BF16),
            pltpu.VMEM((rows, slots * 16), F32),
            pltpu.VMEM((rows, 8, tile), F32),
            pltpu.VMEM((blocks, tile, width), BF16),
            pltpu.VMEM((blocks, tile, width), BF16),
            pltpu.VMEM((rows * tile, width), F32),
            pltpu.VMEM((len(SLOTS), tile + 16, width), BF16),
            pltpu.VMEM((len(SLOTS), tile + 16, width), BF16),
            pltpu.VMEM((16, width, tile), BF16),
            pltpu.VMEM((16, width, tile), F32),
            pltpu.VMEM((16, width, tile), BF16),
            pltpu.VMEM((len(PIECES), width, tile), BF16),
            pltpu.VMEM((len(PIECES), width, tile), BF16),
            pltpu.VMEM((width, width), F32),
            pltpu.VMEM((2, width // 2, width), BF16),
            pltpu.VMEM((width // 2, width), BF16),
            pltpu.VMEM((4, width // 8, width), F32),
            pltpu.VMEM((4, width // 8, width), BF16),
            pltpu.VMEM((4, width // 8, width), BF16),
            pltpu.VMEM((2, width // 16, width), F32),
            pltpu.VMEM((2, width // 16, width), BF16),
            pltpu.VMEM((width // 16, width), BF16),
            pltpu.VMEM((16, 8, tile), F32),
            pltpu.VMEM((16, 8, tile), F32),
            pltpu.SemaphoreType.DMA((rows,)),
            pltpu.SemaphoreType.DMA((N_SEMS,)),
            pltpu.SemaphoreType.DMA((N_SEMS,)),
            pltpu.SemaphoreType.DMA((32,)),
            pltpu.SemaphoreType.DMA((32,)),
        ],
        compiler_params=pltpu.CompilerParams(
            collective_id=0, has_side_effects=True, vmem_limit_bytes=60 * 2**20
        ),
    )(features, reorder, weight, adjacency, tile_block, live_counts, grad_out)
    return pl.pallas_call(
        place_kernel,
        in_specs=[vmem] * 3,
        out_specs=[vmem] * 3,
        out_shape=[jax.ShapeDtypeStruct(a.shape, a.dtype) for a in results],
    )(*results)


def solution(mesh):
    nodes = P(("col", "rep"), None)
    return jax.shard_map(
        on_device,
        mesh=mesh,
        in_specs=(
            nodes,
            nodes,
            P(),
            P("col", "rep", None, None, None, None),
            P("col", "rep", None, None),
            P("col", "rep", None),
            nodes,
        ),
        out_specs=(nodes, nodes, nodes),
        check_vma=False,
    )
```

```python
import math

import jax
import jax.numpy as jnp
from jax import lax
from jax.experimental import pallas as pl
from jax.experimental.pallas import tpu as pltpu
from jax.sharding import PartitionSpec as P

F32, BF16 = jnp.float32, jnp.bfloat16


def dot(a, b):
    return jnp.dot(a, b, preferred_element_type=F32)


OVER_REP = ["y00", "y01"] + [
    d + n
    for d in "pm"
    for n in ("w10", "w11", "w20", "w21", "w30", "w31", "w4", "o20", "o21", "o30", "o31", "o4", "y10", "y11")
]
FORWARD = [f"c{j}" for j in range(8)] + [
    n for m in ("a", "b+", "b-", "k", "d", "e+", "e-") for n in (m + "0", m + "1")
]
BACK = [f"c{j}" for j in range(8)] + [
    n for m in ("x+", "x-", "y", "h", "t", "n+", "n-") for n in (m + "0", m + "1")
]
SETS = [("g", OVER_REP), ("f", FORWARD), ("b", BACK), ("r", OVER_REP)]
INDEX = {n: i for i, n in enumerate(s + n for s, names in SETS for n in names)}
N_SEMS = len(INDEX)
SLOTS = {n: i for i, n in enumerate([f"c{j}" for j in range(8)] + ["a", "b+", "b-", "k", "d", "e+", "e-"])}
PIECES = {n: i for i, n in enumerate(["y0"] + [d + n for d in "pm" for n in ("w1", "w2", "w3", "w4", "o2", "o3", "o4", "y1")])}
PLACES = [(2, 1), (1, 1), (3, 1), (1, 0), (3, 0), (2, 0), (0, 1), (0, 0)]


def layer_kernel(
    feat_ref, order_ref, w_ref, tiles_hbm, block_ref, count_ref, grad_ref,
    act_ref, wgrad_ref, fgrad_ref,
    tiles, slab, ids, degrees, panel, projected, acc, stage_f, land_f, rows_t, totals, totals_low,
    stage_r, land_r, wown, wcore, wcore_in, wmid, wmid_low, wmid_in, wlast, wlast_low, wlast_in,
    wsend2, wland2,
    tile_sem, send_sem, recv_sem, wsend_sem, wrecv_sem,
):
    tile, width = feat_ref.shape
    n_rows, n_slots = tiles.shape[:2]
    c, r = lax.axis_index("col"), lax.axis_index("rep")
    x, yl, core = c // 4, (c // 2) % 2, c % 2
    yh, z = r // 8, r % 8

    def group(dx, dy, dc):
        return ((x + dx) % 4) * 4 + ((yl + dy) % 2) * 2 + (core + dc) % 2

    def block(p, d):
        return ((yh + p) % 2) * 8 + (z + d + 8) % 8

    up, down, over = (c, block(0, 1)), (c, block(0, -1)), (c, block(1, 0))
    right, left, beside = (group(1, 0, 0), r), (group(3, 0, 0), r), (group(0, 1, 0), r)
    partner = (group(0, 0, 1), r)

    def fetch(k):
        return pltpu.make_async_copy(tiles_hbm.at[0, 0, k], tiles.at[k], tile_sem.at[k])

    barrier = pltpu.get_barrier_semaphore()
    for device in (up, down, over, right, left, beside, partner):
        pl.semaphore_signal(barrier, 1, device_id=device)

    @pl.loop(0, n_rows)
    def _(k):
        fetch(k).start()

    def iota(shape, dim):
        return lax.broadcasted_iota(jnp.int32, shape, dim)

    place = (iota((tile, tile), 0) == order_ref[...]).astype(F32)
    own = block(0, 0)
    panel[own] = dot(place.T.astype(BF16), feat_ref[...]).astype(BF16)

    n_blocks, strip = slab.shape[0], 16
    wide = n_slots * strip
    spread = (iota((n_slots, wide), 1) // strip == iota((n_slots, wide), 0)).astype(BF16)
    ids[...] = dot(block_ref[0, 0].astype(F32).astype(BF16), spread)

    def build(k):
        fetch(k).wait()
        shape = (n_blocks * strip + strip, wide)
        out_at, in_at = iota(shape, 0), iota(shape, 1)
        picked = (ids[pl.ds(k, 1), :] == (out_at // strip).astype(F32)) | (out_at >= n_blocks * strip)
        live = in_at // strip < count_ref[0, 0, k]
        pick = picked & live & (out_at % strip == in_at % strip)
        pick = jnp.where(pick, 1.0, 0.0).astype(BF16)
        slots = jnp.concatenate(
            [tiles[k, :, g * strip : (g + 1) * strip, :].reshape(wide, tile) for g in range(tile // strip)],
            axis=1,
        )
        out = dot(pick, slots)

        def rows_of(b):
            part = out[b * strip : (b + 1) * strip]
            return jnp.concatenate(
                [part[:, g * tile : (g + 1) * tile] for g in range(tile // strip)], axis=0
            )

        rows = pl.ds(pl.multiple_of(k * tile, tile), tile)
        for b in range(n_blocks):
            slab[b, rows] = rows_of(b).astype(BF16)
        degrees[k] = jnp.broadcast_to(
            jnp.sum(rows_of(n_blocks).T, axis=0, keepdims=True), degrees.shape[1:]
        )

    pl.loop(0, n_rows // 2)(build)
    pl.semaphore_wait(barrier, 7)
    copies = {}

    def send(name, src, dst, device):
        i = INDEX[name]
        copy = pltpu.make_async_remote_copy(
            src, dst, send_sem.at[i], recv_sem.at[i], device_id=device
        )
        copy.start()
        copies[name] = copy

    def arrived(name):
        copies[name].wait_recv()

    half = tile // 2

    def pass_on(name, p, d, device, h):
        ref = panel.at[block(p, d), pl.ds(h * half, half)]
        send("g" + name, ref, ref, device)

    def consume(b1, b2, first=False):
        for b in (b1, b2):
            projected[b] = dot(panel[b], w_ref[...]).astype(BF16)
        pair = jnp.concatenate([projected[b1], projected[b2]], axis=0)

        @pl.loop(0, slab.shape[1] // 512)
        def _(i):
            rows = pl.ds(pl.multiple_of(i * 512, 512), 512)
            part = dot(jnp.concatenate([slab[b1, rows], slab[b2, rows]], axis=1), pair)
            acc[rows] = part if first else acc[rows] + part

    ways = (("p", -1, up, 0), ("m", 1, down, 1))
    for h in (0, 1):
        for way, s, device, _ in ways:
            pass_on(f"{way}w1{h}", 0, 0, device, h)
        pass_on(f"y0{h}", 0, 0, over, h)
    pl.loop(n_rows // 2, n_rows)(build)
    for h in (0, 1):
        for way, s, device, _ in ways:
            arrived(f"g{way}w1{h}")
            pass_on(f"{way}w2{h}", 0, s, device, h)
            pass_on(f"{way}y1{h}", 0, s, over, h)
    for h in (0, 1):
        arrived(f"gy0{h}")
    consume(own, block(1, 0), first=True)
    for h in (0, 1):
        for way, s, device, _ in ways:
            arrived(f"g{way}w2{h}")
            pass_on(f"{way}w3{h}", 0, 2 * s, device, h)
    consume(block(0, 1), block(0, -1))
    for h in (0, 1):
        for way, s, device, _ in ways:
            arrived(f"g{way}y1{h}")
            pass_on(f"{way}o2{h}", 1, s, device, h)
    consume(block(0, 2), block(0, -2))
    for way, s, device, e in ways:
        arrived(f"g{way}w3{e}")
        pass_on(f"{way}w4", 0, 3 * s, device, e)
    consume(block(1, 1), block(1, -1))
    for h in (0, 1):
        for way, s, device, e in ways:
            arrived(f"g{way}o2{(h + e) % 2}")
            pass_on(f"{way}o3{(h + e) % 2}", 1, 2 * s, device, (h + e) % 2)
    for way, s, device, e in ways:
        arrived(f"g{way}w3{1 - e}")
    consume(block(0, 3), block(0, -3))
    for way, s, device, e in ways:
        arrived(f"g{way}o3{e}")
        pass_on(f"{way}o4", 1, 3 * s, device, e)
    consume(block(1, 2), block(1, -2))
    for way, s, device, e in ways:
        arrived(f"g{way}o3{1 - e}")
        arrived(f"g{way}w4")
    consume(block(1, 3), block(1, -3))
    for way, s, device, e in ways:
        arrived(f"g{way}o4")
    consume(block(0, 4), block(1, 4))

    def span(h):
        return slice(h * half, tile + 16 * h if h else half)

    def mine(dx, dy, dc, h):
        k = group(dx, dy, dc)
        rows = acc[pl.ds(pl.multiple_of(k * tile + h * half, half), half)]
        return rows, degrees[k][0:1]

    def pack(name, h, value):
        slot, (rows, degree) = SLOTS[name], value
        stage_f[slot, h * half : (h + 1) * half] = rows.astype(BF16)
        if h:
            high = degree.astype(BF16)
            low = (degree - high.astype(F32)).astype(BF16)
            none = jnp.zeros_like(high)
            stage_f[slot, tile : tile + 16] = jnp.concatenate(
                [jnp.broadcast_to(part, (16, tile)) for part in (high, low, none, none)], axis=1
            )

    def plus(value, name, h):
        slot, (rows, degree) = SLOTS[name], value
        rows = rows + land_f[slot, h * half : (h + 1) * half].astype(F32)
        if h:
            tail = land_f[slot, tile : tile + 16].astype(F32)
            degree = degree + tail[0:1, 0:tile] + tail[0:1, tile : 2 * tile]
        return rows, degree

    def ship(name, h, device):
        slot = SLOTS[name]
        at = pl.ds(span(h).start, span(h).stop - span(h).start)
        send(f"f{name}{h}", stage_f.at[slot, at], land_f.at[slot, at], device)

    for j, (dx, dy) in enumerate(PLACES):
        for h in (0, 1):
            pack(f"c{j}", h, mine(dx, dy, 1, h))
        send(f"fc{j}", stage_f.at[j], land_f.at[j], partner)

    def both(dx, dy, h):
        return plus(mine(dx, dy, 0, h), f"c{PLACES.index((dx, dy))}", h)

    def go(name, h, value, device):
        pack(name, h, value)
        ship(name, h, device)

    sides = (("+", 1, right, 0), ("-", 3, left, 1))
    arrived("fc0")
    for h in (0, 1):
        go("a", h, both(2, 1, h), beside)
    for j, (s, dx, device, e) in enumerate(sides):
        arrived(f"fc{1 + j}")
        go("b" + s, e, both(dx, 1, e), device)
        go("b" + s, 1 - e, both(dx, 1, 1 - e), device)
    for j, (s, dx, device, e) in enumerate(sides):
        arrived(f"fc{3 + j}")
        go("e" + s, 1 - e, both(dx, 0, 1 - e), device)
    arrived("fc5")
    for s, dx, device, e in sides:
        arrived(f"fa{e}")
        go("k", e, plus(both(2, 0, e), "a", e), device)
    arrived("fc6")
    for h in (0, 1):
        arrived(f"fb+{h}")
        arrived(f"fb-{h}")
        go("d", h, plus(plus(both(0, 1, h), "b+", h), "b-", h), beside)
    for s, dx, device, e in sides:
        arrived(f"fk{e}")
        go("e" + s, e, plus(both(dx, 0, e), "k", e), device)
    arrived("fc7")
    parts = []
    for h in (0, 1):
        value = both(0, 0, h)
        for name in ("d", "e+", "e-"):
            arrived(f"f{name}{h}")
            value = plus(value, name, h)
        parts.append(value)
    summed = jnp.concatenate([parts[0][0], parts[1][0]], axis=0)
    degree = parts[1][1]

    scale = lax.rsqrt(1.0 + jnp.broadcast_to(degree, (tile, tile)).T)
    scale = jnp.concatenate([scale] * (width // tile), axis=1)
    pre_act = summed * scale + projected[own].astype(F32)
    sigmoid = 1.0 / (1.0 + jnp.exp(-pre_act))
    pre_grad = grad_ref[...].astype(F32) * sigmoid * (1.0 + pre_act * (1.0 - sigmoid))
    rows_t[c] = (pre_grad * scale).T.astype(BF16)

    middle = width // 2

    def hand(name, dx, dy, device, h):
        ref = rows_t.at[group(dx, dy, 0), pl.ds(h * middle, middle)]
        send("b" + name, ref, ref, device)

    def to_partner(dx, dy):
        ref = rows_t.at[group(dx, dy, 0)]
        send(f"bc{PLACES.index((dx, dy))}", ref, ref, partner)

    for h in (0, 1):
        for s, dx, device, e in sides:
            hand(f"x{s}{(h + e) % 2}", 0, 0, device, (h + e) % 2)
        hand(f"y{h}", 0, 0, beside, h)
    to_partner(0, 0)
    pre_grad_t = pre_grad.T
    act_ref[...] = (pre_act * sigmoid).astype(BF16)
    for s, dx, device, e in sides:
        arrived(f"bx{s}{e}")
        hand(f"h{e}", 4 - dx, 0, device, e)
    for h in (0, 1):
        arrived(f"by{h}")
        for s, dx, device, e in sides:
            hand(f"n{s}{h}", 0, 1, device, h)
    for s, dx, device, e in sides:
        arrived(f"bx{s}{1 - e}")
        to_partner(4 - dx, 0)
    to_partner(0, 1)
    for e in (0, 1):
        arrived(f"bh{e}")
        hand(f"t{e}", 2, 0, beside, e)
    to_partner(2, 0)
    for s, dx, device, e in sides:
        arrived(f"bn{s}0")
        arrived(f"bn{s}1")
        to_partner(4 - dx, 1)
    arrived("bt0")
    arrived("bt1")
    to_partner(2, 1)
    for j in range(8):
        arrived(f"bc{j}")

    def column_sums(b1, b2):
        left_side = jnp.concatenate([rows_t[k] for k in range(rows_t.shape[0])], axis=1)
        sums = dot(left_side, jnp.concatenate([slab[b1], slab[b2]], axis=1))
        for b, part in ((b1, sums[:, :tile]), (b2, sums[:, tile:])):
            totals[b] = part
            totals_low[b] = part.astype(BF16)

    ways = (("m", -1, down, 0), ("p", 1, up, 1))

    def leaf(name, h, p, d, device, one=False):
        at = pl.ds(h * middle, middle)
        src, dst = totals_low.at[block(p, d), at], land_r.at[PIECES[name], at]
        send(f"r{name}" if one else f"r{name}{h}", src, dst, device)

    def join(name, children, h, p, d, device):
        at, slot = pl.ds(h * middle, middle), PIECES[name]
        value = totals[block(p, d), at]
        for child in children:
            arrived(f"r{child}" if child[1:] in ("w4", "o4") else f"r{child}{h}")
            value = value + land_r[PIECES[child], at].astype(F32)
        stage_r[slot, at] = value.astype(BF16)
        send(f"r{name}{h}", stage_r.at[slot, at], land_r.at[slot, at], device)

    column_sums(block(0, 4), block(1, 4))
    for way, s, device, e in ways:
        leaf(way + "o4", e, 1, 4, device, one=True)
    for way, s, device, e in ways:
        leaf(way + "w4", e, 0, 4, device, one=True)
    column_sums(block(1, 3), block(1, -3))
    for way, s, device, e in ways:
        leaf(way + "o3", 1 - e, 1, 3 * s, device)
    column_sums(block(0, 3), block(0, -3))
    for way, s, device, e in ways:
        leaf(way + "w3", 1 - e, 0, 3 * s, device)
    column_sums(block(1, 0), own)
    for h in (0, 1):
        leaf("y0", h, 1, 0, over)
    column_sums(block(1, 2), block(1, -2))
    for way, s, device, e in ways:
        join(way + "o3", [way + "o4"], e, 1, 3 * s, device)
    for way, s, device, e in ways:
        join(way + "w3", [way + "w4"], e, 0, 3 * s, device)
    column_sums(block(1, 1), block(1, -1))
    for way, s, device, e in ways:
        join(way + "o2", [way + "o3"], 1 - e, 1, 2 * s, device)
    column_sums(block(0, 2), block(0, -2))
    column_sums(block(0, 1), block(0, -1))
    for way, s, device, e in ways:
        join(way + "o2", [way + "o3"], e, 1, 2 * s, device)
    for way, s, device, e in ways:
        join(way + "w2", [way + "w3"], 1 - e, 0, 2 * s, device)

    blocks = range(panel.shape[0])
    slim = width // 16
    grad_low = pre_grad_t.astype(BF16)
    wcopies = {}

    def wsend(name, i, src, dst, device):
        copy = pltpu.make_async_remote_copy(
            src, dst, wsend_sem.at[i], wrecv_sem.at[i], device_id=device
        )
        copy.start()
        wcopies[name] = copy

    for i in range(width // tile):
        columns = slice(i * tile, (i + 1) * tile)
        term = dot(
            jnp.concatenate([totals_low[b] for b in blocks] + [grad_low], axis=1),
            jnp.concatenate(
                [panel[b, :, columns] for b in blocks] + [panel[own][:, columns]], axis=0
            ),
        ).T
        wown[columns] = term
        for j in range(tile // slim):
            rows = term[j * slim : (j + 1) * slim].astype(BF16)
            wcore[j % 2, pl.ds((i * 2 + j // 2) * slim, slim)] = rows
    wsend("core", 0, wcore.at[1 - core], wcore_in, partner)

    wcopies["core"].wait_recv()
    for i in range(4):
        for j in range(2):
            at = pl.ds((i * 2 + j) * slim, slim)
            rows = wown[pl.ds(pl.multiple_of((i * 4 + j * 2 + core) * slim, slim), slim)]
            rows = rows + wcore_in[at].astype(F32)
            wmid[i, pl.ds(j * slim, slim)] = rows
            wmid_low[i, pl.ds(j * slim, slim)] = rows.astype(BF16)
    for i in range(1, 4):
        wsend(f"x{i}", i, wmid_low.at[(x + i) % 4], wmid_in.at[i], (group(i, 0, 0), r))
    for way, s, device, e in ways:
        join(way + "y1", [way + "o2"], 1 - e, 1, s, over)
    for way, s, device, e in ways:
        join(way + "w2", [way + "w3"], e, 0, 2 * s, device)
    for way, s, device, e in ways:
        join(way + "y1", [way + "o2"], e, 1, s, over)
    pair = wmid[x]
    for i in range(1, 4):
        wcopies[f"x{i}"].wait_recv()
        pair = pair + wmid_in[i].astype(F32)
    for j in range(2):
        wlast[j] = pair[j * slim : (j + 1) * slim]
        wlast_low[j] = pair[j * slim : (j + 1) * slim].astype(BF16)
    wsend("y", 4, wlast_low.at[1 - yl], wlast_in, beside)
    for way, s, device, e in ways:
        join(way + "w1", [way + "w2", way + "y1"], 1 - e, 0, s, device)
    for way, s, device, e in ways:
        join(way + "w1", [way + "w2", way + "y1"], e, 0, s, device)
    wcopies["y"].wait_recv()
    total = wlast[yl] + wlast_in[...].astype(F32)
    two, lanes = slim // 16, tile
    for i in range(16):
        rows = total[i * two : (i + 1) * two]
        wsend2[i] = jnp.concatenate(
            [rows[:, q * lanes : (q + 1) * lanes] for q in range(width // lanes)], axis=0
        )
    for i in range(1, 16):
        to = lax.rem(r + i, 16)
        wsend(f"r{i}", 16 + i, wsend2.at[to], wland2.at[i], (c, to))

    back = []
    for h in (0, 1):
        at = pl.ds(h * middle, middle)
        value = totals[own, at] + pre_grad_t[h * middle : (h + 1) * middle]
        for name in ("y0", "mw1", "pw1"):
            arrived(f"r{name}{h}")
            value = value + land_r[PIECES[name], at].astype(F32)
        back.append(value)
    back = jnp.concatenate(back, axis=0).T.astype(BF16)
    input_rows = lax.dot_general(
        back, w_ref[...], (((1,), (1,)), ((), ())), preferred_element_type=F32
    ).astype(BF16)
    fgrad_ref[...] = dot(place.astype(BF16), input_rows).astype(BF16)

    pair = wsend2[r]
    for i in range(1, 16):
        wcopies[f"r{i}"].wait_recv()
        pair = pair + wland2[i]
    pair = jnp.concatenate([pair[q * two : (q + 1) * two] for q in range(width // lanes)], axis=1)
    wgrad_ref[...] = pair * (1.0 / math.sqrt(tile * 256))
    for copy in [*copies.values(), *wcopies.values()]:
        copy.wait_send()


def place_kernel(*refs):
    for src, dst in zip(refs[: len(refs) // 2], refs[len(refs) // 2 :], strict=True):
        dst[...] = src[...]


def on_device(features, reorder, weight, adjacency, tile_block, live_counts, grad_out):
    tile, width = features.shape
    _, _, rows, slots, _, _ = adjacency.shape
    blocks = 16
    vmem = pl.BlockSpec(memory_space=pltpu.VMEM)
    results = pl.pallas_call(
        layer_kernel,
        in_specs=[
            vmem, vmem, vmem, pl.BlockSpec(memory_space=pl.ANY), vmem,
            pl.BlockSpec(memory_space=pltpu.SMEM), vmem,
        ],
        out_specs=[vmem, vmem, vmem],
        out_shape=[
            jax.ShapeDtypeStruct((tile, width), BF16),
            jax.ShapeDtypeStruct((width // 256, width), F32),
            jax.ShapeDtypeStruct((tile, width), BF16),
        ],
        scratch_shapes=[
            pltpu.VMEM((rows, slots, tile, tile), BF16),
            pltpu.VMEM((blocks, rows * tile, tile), BF16),
            pltpu.VMEM((rows, slots * 16), F32),
            pltpu.VMEM((rows, 8, tile), F32),
            pltpu.VMEM((blocks, tile, width), BF16),
            pltpu.VMEM((blocks, tile, width), BF16),
            pltpu.VMEM((rows * tile, width), F32),
            pltpu.VMEM((len(SLOTS), tile + 16, width), BF16),
            pltpu.VMEM((len(SLOTS), tile + 16, width), BF16),
            pltpu.VMEM((16, width, tile), BF16),
            pltpu.VMEM((16, width, tile), F32),
            pltpu.VMEM((16, width, tile), BF16),
            pltpu.VMEM((len(PIECES), width, tile), BF16),
            pltpu.VMEM((len(PIECES), width, tile), BF16),
            pltpu.VMEM((width, width), F32),
            pltpu.VMEM((2, width // 2, width), BF16),
            pltpu.VMEM((width // 2, width), BF16),
            pltpu.VMEM((4, width // 8, width), F32),
            pltpu.VMEM((4, width // 8, width), BF16),
            pltpu.VMEM((4, width // 8, width), BF16),
            pltpu.VMEM((2, width // 16, width), F32),
            pltpu.VMEM((2, width // 16, width), BF16),
            pltpu.VMEM((width // 16, width), BF16),
            pltpu.VMEM((16, 8, tile), F32),
            pltpu.VMEM((16, 8, tile), F32),
            pltpu.SemaphoreType.DMA((rows,)),
            pltpu.SemaphoreType.DMA((N_SEMS,)),
            pltpu.SemaphoreType.DMA((N_SEMS,)),
            pltpu.SemaphoreType.DMA((32,)),
            pltpu.SemaphoreType.DMA((32,)),
        ],
        compiler_params=pltpu.CompilerParams(
            collective_id=0, has_side_effects=True, vmem_limit_bytes=60 * 2**20
        ),
    )(features, reorder, weight, adjacency, tile_block, live_counts, grad_out)
    return pl.pallas_call(
        place_kernel,
        in_specs=[vmem] * 3,
        out_specs=[vmem] * 3,
        out_shape=[jax.ShapeDtypeStruct(a.shape, a.dtype) for a in results],
    )(*results)


def solution(mesh):
    nodes = P(("col", "rep"), None)
    return jax.shard_map(
        on_device,
        mesh=mesh,
        in_specs=(
            nodes,
            nodes,
            P(),
            P("col", "rep", None, None, None, None),
            P("col", "rep", None, None),
            P("col", "rep", None),
            nodes,
        ),
        out_specs=(nodes, nodes, nodes),
        check_vma=False,
    )
```
